32 devices in a mesh: gx: 8 (over z, x), gy: 4 (over y, core).
Axes of the slice: x: 2, y: 2, z: 4, core: 2. Of those that a mesh axis runs over, the one named last changes fastest.
Arguments:
- velocity: float32 [128, 3, 4, 16384], P('gx', None, None, 'gy'), may hold values from -6 to 6
- metric_x: float32 [128], P('gx'), may hold values from 0.5 to 2
- metric_y: float32 [16384], P('gy'), may hold values from 0.5 to 2
Outputs:
- deriv_x: float32 [128, 3, 4, 16384], P('gx', None, None, 'gy')
- deriv_y: float32 [128, 3, 4, 16384], P('gx', None, None, 'gy')
The draws below stay inside these ranges and needn't reach their ends.
All inputs are finite; a program needn't handle non-finite values.
Results may differ from the reference program's by a relative error of at most 0.00007.
Values sent between devices are 32-bit elements; how exact they have to be, the bound alone decides.
A program may use at most 256 MiB of HBM per device.

```python
import math
import jax
import jax.numpy as jnp
from jax import lax

NZ = 4
NX = 128
NY = 16384


def levels(rng, shape, cuts, least, top_value):
    level, own = 1.0, jax.random.fold_in(rng, 6)
    for axis_at, blocks in cuts:
        heights = jnp.exp(jax.random.uniform(jax.random.fold_in(own, axis_at), (blocks,), jnp.float32, least / len(cuts), top_value / len(cuts)))
        level = level * jnp.repeat(heights, shape[axis_at] // blocks).reshape([-1 if axis == axis_at else 1 for axis in range(len(shape))])
    return level


def gaussian(own_key, shape, width, bound, pieces=(), kind=jnp.bfloat16):
    drawn = width * jax.random.normal(own_key, shape, jnp.float32)
    if pieces:
        drawn = drawn * levels(own_key, shape, pieces, -0.22, 0.18)
    return jnp.clip(drawn, -bound, bound).astype(kind)


def setup_inputs(seed: int = 0) -> dict:
    key_of = jax.random.split(jax.random.key(seed), 4)
    velocity = gaussian(key_of[0], (NX, 3, NZ, NY), 1.0, 6.0, ((0, 8), (3, 4)), jnp.float32)
    metric_x = jnp.clip(jnp.exp(math.log(2.0) - 1.3862944 * jax.random.uniform(key_of[1], (NX,), jnp.float32) ** levels(key_of[1], (NX,), ((0, 8),), -0.2, 0.2)), 0.5, 2.0)
    metric_y = jnp.clip(jnp.exp(math.log(2.0) - 1.3862944 * jax.random.uniform(key_of[2], (NY,), jnp.float32) ** levels(key_of[2], (NY,), ((0, 4),), -0.2, 0.2)), 0.5, 2.0)
    return dict(velocity=velocity, metric_x=metric_x, metric_y=metric_y)


ALPHA = 0.49
NEAR = 949.0 / 1200.0
MID = 167.0 / 1500.0
FAR = -47.0 / 6000.0


def periodic_derivative(field, axis, length):
    rhs = NEAR * (jnp.roll(field, -1, axis) - jnp.roll(field, 1, axis))
    rhs = rhs + MID * (jnp.roll(field, -2, axis) - jnp.roll(field, 2, axis))
    rhs = rhs + FAR * (jnp.roll(field, -3, axis) - jnp.roll(field, 3, axis))
    wave = jnp.arange(length // 2 + 1).astype(field.dtype)
    denom = 1.0 + 2.0 * ALPHA * jnp.cos(2.0 * math.pi * wave / length)
    shape = [1, 1]
    shape[axis] = length // 2 + 1
    spectrum = jnp.fft.rfft(rhs, axis=axis) / denom.reshape(shape)
    return jnp.fft.irfft(spectrum, n=length, axis=axis).astype(field.dtype)


def reference(velocity, metric_x, metric_y):
    stacked = jnp.transpose(velocity, (1, 2, 0, 3)).reshape(3 * NZ, NX, NY)

    def one_plane(field):
        along_x = periodic_derivative(field, 0, NX) * metric_x[:, None]
        along_y = periodic_derivative(field, 1, NY) * metric_y[None, :]
        return along_x, along_y

    deriv_x, deriv_y = lax.map(one_plane, stacked)
    deriv_x = jnp.transpose(deriv_x.reshape(3, NZ, NX, NY), (2, 0, 1, 3))
    deriv_y = jnp.transpose(deriv_y.reshape(3, NZ, NX, NY), (2, 0, 1, 3))
    return deriv_x, deriv_y
```

```python
import functools
import math

import jax
import jax.numpy as jnp
import numpy as np
from jax import lax
from jax.experimental import pallas as pl
from jax.experimental.pallas import tpu as pltpu
from jax.sharding import PartitionSpec as P

ALPHA = 0.49
COEF = {1: 949.0 / 1200.0, 2: 167.0 / 1500.0, 3: -47.0 / 6000.0}
RATIO = (1.0 - math.sqrt(1.0 - 4.0 * ALPHA * ALPHA)) / (2.0 * ALPHA)
RHO = -RATIO
LEADING = 1.0 / (1.0 - 2.0 * ALPHA * RATIO)
MESH = pl.DeviceIdType.MESH
TILE = 128


def power(count):
    return float(RHO**count)


def response(offset):
    green = lambda n: LEADING * RHO ** abs(n)
    return sum(w * (green(offset - k) - green(offset + k)) for k, w in COEF.items())


WAVE = response(3) / RHO**2
BAND1 = response(1) - WAVE
BAND2 = response(2) - WAVE * RHO


def y_tables():
    own, up, down = (np.zeros((TILE, TILE)) for _ in range(3))
    for j in range(TILE):
        for l in range(TILE):
            own[j, l] = response(j - l)
            up[j, l] = response(j - TILE - l)
            down[j, l] = response(j + TILE - l)
    table = np.concatenate((own, up, down), 1)
    high = table.astype(jnp.bfloat16)
    low = (table - high.astype(np.float64)).astype(jnp.bfloat16)
    return np.concatenate((high, high, low), 0)


def edge_weights(cells):
    away = np.arange(cells, dtype=np.float64)
    return np.stack((RHO**away, RHO ** (cells - 1 - away))).astype(np.float32)


def exchange(nx, ny, v, wy, ein, halo, ygot, vbuf, esend, erecv, ssend, first, last, ysend,
             load_sem, edge_sem, own_sem, halo_send, halo_recv, e_s, e_r, s_s, s_r, y_s, y_r):
    cells, comps, planes, columns = v.shape
    width = columns // nx
    x, y = lax.axis_index("gx"), lax.axis_index("gy")

    def target(q):
        return lax.rem(x + 1 + q, nx)

    def load(q):
        at = pl.multiple_of(target(q) * width, TILE)
        return pltpu.make_async_copy(v.at[:, :, :, pl.ds(at, width)], vbuf.at[q % 2], load_sem.at[q % 2])

    load(0).start()
    edges = [
        pltpu.make_async_copy(v.at[:, :, :, pl.ds(0, TILE)], first, edge_sem.at[0]),
        pltpu.make_async_copy(v.at[:, :, :, pl.ds(columns - TILE, TILE)], last, edge_sem.at[1]),
    ]
    for copy in edges:
        copy.start()
    barrier = pltpu.get_barrier_semaphore()
    for q in range(nx - 1):
        pl.semaphore_signal(barrier, inc=1, device_id=(target(q), y), device_id_type=MESH)
    for q in range(ny - 1):
        pl.semaphore_signal(barrier, inc=1, device_id=(x, lax.rem(y + 1 + q, ny)), device_id_type=MESH)
    pl.semaphore_wait(barrier, nx + ny - 2)

    right, left = lax.rem(x + 1, nx), lax.rem(x + nx - 1, nx)
    rims = [
        pltpu.make_async_remote_copy(
            v.at[pl.ds(cells - 2, 2)], halo.at[0], halo_send.at[0], halo_recv.at[0],
            device_id=(right, y), device_id_type=MESH),
        pltpu.make_async_remote_copy(
            v.at[pl.ds(0, 2)], halo.at[1], halo_send.at[1], halo_recv.at[1],
            device_id=(left, y), device_id_type=MESH),
    ]
    for copy in rims:
        copy.start()

    sends = []
    to_low = jnp.zeros((cells, comps, planes, TILE), jnp.float32)
    to_high = jnp.zeros((cells, comps, planes, TILE), jnp.float32)
    ysum = [to_low, to_high]
    for q in range(nx):
        load(q).wait()
        if q + 1 < nx:
            load(q + 1).start()
        block = vbuf.at[q % 2]
        goes = esend.at[q] if q < nx - 1 else erecv.at[q]
        low, high = block[cells - 1], block[0]
        for i in range(1, cells):
            low = block[cells - 1 - i] + RHO * low
            high = block[i] + RHO * high
        goes[0] = low
        goes[1] = high
        if q < nx - 1:
            copy = pltpu.make_async_remote_copy(
                esend.at[q], erecv.at[q], e_s.at[q], e_r.at[q],
                device_id=(target(q), y), device_id_type=MESH)
            copy.start()
            sends.append(copy)
        start = target(q) * width
        for t in range(width // TILE):
            at = pl.multiple_of(start + t * TILE, TILE)
            part = block[:, :, :, t * TILE : (t + 1) * TILE]
            for side in range(2):
                ysum[side] = ysum[side] + part * wy[pl.ds(side, 1), pl.ds(at, TILE)][None, None]

    for copy in edges:
        copy.wait()
    lane = lax.broadcasted_iota(jnp.int32, (cells, comps, planes, TILE), 3)
    sums = [jnp.sum(part, axis=3, keepdims=True) for part in ysum]
    message = jnp.where(lane < 2, first[...], jnp.where(lane >= TILE - 2, last[...], 0.0))
    message = jnp.where(lane == 2, sums[0], jnp.where(lane == 3, sums[1], message))
    ysend[...] = message
    for q in range(ny - 1):
        copy = pltpu.make_async_remote_copy(
            ysend, ygot.at[q], y_s.at[q], y_r.at[q],
            device_id=(x, lax.rem(y + 1 + q, ny)), device_id_type=MESH)
        copy.start()
        sends.append(copy)
    own_y = pltpu.make_async_copy(ysend, ygot.at[ny - 1], own_sem.at[0])
    own_y.start()

    for copy in sends[: nx - 1]:
        copy.wait_recv()
    closing = 1.0 / (1.0 - power(cells * nx))
    spot = pl.multiple_of(x * width, TILE)
    for q in range(nx):
        from_low, from_high = 0.0, 0.0
        for s in range(nx):
            ahead = (q + s + 1) % nx + 1
            behind = (-(q + s + 2) - 1) % nx + 1
            from_low = from_low + closing * power(cells * (ahead - 1)) * erecv[s, 1]
            from_high = from_high + closing * power(cells * (behind - 1)) * erecv[s, 0]
        ssend[q, 0] = from_low
        ssend[q, 1] = from_high
        place = ein.at[:, :, :, pl.ds(spot, width)]
        if q < nx - 1:
            copy = pltpu.make_async_remote_copy(
                ssend.at[q], place, s_s.at[q], s_r.at[q],
                device_id=(target(q), y), device_id_type=MESH)
            copy.start()
            sends.append(copy)
        else:
            own_x = pltpu.make_async_copy(ssend.at[q], place, own_sem.at[1])
            own_x.start()
    own_y.wait()
    own_x.wait()
    for copy in rims:
        copy.wait()
    for copy in sends[: nx - 1]:
        copy.wait_send()
    for copy in sends[nx - 1 : nx + ny - 2]:
        copy.wait()
    for q, copy in enumerate(sends[nx + ny - 2 :]):
        copy.wait_send()
        at = pl.multiple_of(lax.rem(x + nx - 1 - q, nx) * width, TILE)
        pltpu.make_async_remote_copy(
            ssend.at[q], ein.at[:, :, :, pl.ds(at, width)], s_s.at[q], s_r.at[q],
            device_id=(target(q), y), device_id_type=MESH).wait_recv()


def derive(ny, mx, v, ein, halo, ygot, my, table, dx, dy, lhs, prod):
    cells, _, planes, columns = v.shape
    lines = cells * planes
    tiles = columns // TILE

    def flat(part):
        return part.reshape(lines, TILE)

    group = min(8, tiles)

    @pl.loop(0, tiles // group)
    def _(g):
        for t in range(group):
            at = pl.multiple_of((g * group + t) * TILE, TILE)
            part = flat(v[:, 0, :, pl.ds(at, TILE)])
            high = part.astype(jnp.bfloat16)
            low = (part - high.astype(jnp.float32)).astype(jnp.bfloat16)
            lhs[t * lines : (t + 1) * lines, 0:TILE] = high
            lhs[t * lines : (t + 1) * lines, TILE : 2 * TILE] = low
            lhs[t * lines : (t + 1) * lines, 2 * TILE :] = high
        rows = group * lines
        prod[pl.ds(pl.multiple_of(g * rows, rows), rows), :] = jnp.dot(
            lhs[...], table[...], preferred_element_type=jnp.float32)

    wide = 2 * TILE

    @pl.loop(0, columns // wide)
    def _(g):
        at = pl.ds(pl.multiple_of(g * wide, wide), wide)
        row = lambda i: (
            v[i, 0, :, at] if 0 <= i < cells
            else halo[0, 2 + i, 0, :, at] if i < 0
            else halo[1, i - cells, 0, :, at])
        above = [None] * cells
        above[cells - 1] = ein[1, 0, :, at]
        for i in range(cells - 1, 0, -1):
            above[i - 1] = row(i) + RHO * above[i]
        below = ein[0, 0, :, at]
        for i in range(cells):
            line = WAVE * (above[i] - below) + BAND1 * (row(i + 1) - row(i - 1))
            line = line + BAND2 * (row(i + 2) - row(i - 2))
            dx[i, 0, :, at] = mx[i] * line
            below = row(i) + RHO * below

    lane = lax.broadcasted_iota(jnp.int32, (1, TILE), 1)
    away = lane.astype(jnp.float32)
    sign = jnp.where(lane % 2 == 0, 1.0, -1.0).astype(jnp.float32)
    rise = WAVE * sign * jnp.exp(away * math.log(RATIO))
    fall = WAVE * -sign * jnp.exp((TILE - 1 - away) * math.log(RATIO))
    fall = -fall if TILE % 2 else fall
    step = power(columns)
    closing = 1.0 / (1.0 - power(columns * ny))
    low_in, high_in = 0.0, 0.0
    for s in range(ny):
        got = flat(ygot[s, :, 0])
        ahead = s + 1
        behind = ny - 1 - s if s < ny - 1 else ny
        low_in = low_in + closing * step ** (ahead - 1) * got[:, 3:4]
        high_in = high_in + closing * step ** (behind - 1) * got[:, 2:3]
    before = flat(ygot[0, :, 0])[:, TILE - 2 :]
    after = flat(ygot[ny - 2, :, 0])[:, 0:2]
    jump = power(TILE)

    def at_lane(n, value):
        return jnp.where(lane == n, value, 0.0)

    highs = [None] * tiles
    far = high_in
    for k in range(tiles - 1, -1, -1):
        highs[k] = far
        if k:
            seen = prod[k * lines : (k + 1) * lines, 3 * TILE - 3 : 3 * TILE - 2]
            far = seen * (1.0 / (WAVE * RHO**2)) + jump * far
    far = low_in
    for k in range(tiles):
        rows = slice(k * lines, (k + 1) * lines)
        line = prod[rows, 0:TILE]
        if k:
            line = line + prod[(k - 1) * lines : k * lines, TILE : 2 * TILE]
            line = line - (jump * past) * rise
        else:
            line = line - far * rise
            line = line - at_lane(0, BAND1 * before[:, 1:2] + BAND2 * before[:, 0:1])
            line = line - at_lane(1, BAND2 * before[:, 1:2])
        if k < tiles - 1:
            line = line + prod[(k + 1) * lines : (k + 2) * lines, 2 * TILE :]
            line = line + (jump * highs[k + 1]) * fall
        else:
            line = line + highs[k] * fall
            line = line + at_lane(TILE - 1, BAND1 * after[:, 0:1] + BAND2 * after[:, 1:2])
            line = line + at_lane(TILE - 2, BAND2 * after[:, 0:1])
        at = slice(k * TILE, (k + 1) * TILE)
        dy[:, 0, :, at] = (line * my[:, at]).reshape(cells, planes, TILE)
        past = far
        seen = prod[rows, TILE + 2 : TILE + 3]
        far = seen * (-1.0 / (WAVE * RHO**2)) + jump * past


def body(nx, ny, velocity, metric_x, metric_y):
    cells, comps, planes, columns = velocity.shape
    width = columns // nx
    f32 = jnp.float32
    dma = pltpu.SemaphoreType.DMA
    hbm = pl.BlockSpec(memory_space=pl.ANY)
    ein, halo, ygot = pl.pallas_call(
        functools.partial(exchange, nx, ny),
        out_shape=[
            jax.ShapeDtypeStruct((2, comps, planes, columns), f32),
            jax.ShapeDtypeStruct((2, 2, comps, planes, columns), f32),
            jax.ShapeDtypeStruct((ny, cells, comps, planes, TILE), f32),
        ],
        in_specs=[hbm, pl.BlockSpec(memory_space=pltpu.VMEM)],
        out_specs=[hbm, hbm, hbm],
        scratch_shapes=[
            pltpu.VMEM((2, cells, comps, planes, width), f32),
            pltpu.VMEM((nx, 2, comps, planes, width), f32),
            pltpu.VMEM((nx, 2, comps, planes, width), f32),
            pltpu.VMEM((nx, 2, comps, planes, width), f32),
            pltpu.VMEM((cells, comps, planes, TILE), f32),
            pltpu.VMEM((cells, comps, planes, TILE), f32),
            pltpu.VMEM((cells, comps, planes, TILE), f32),
            dma((2,)), dma((2,)), dma((2,)), dma((2,)), dma((2,)),
            dma((nx,)), dma((nx,)), dma((nx,)), dma((nx,)), dma((ny,)), dma((ny,)),
        ],
        compiler_params=pltpu.CompilerParams(
            collective_id=0, has_side_effects=True, vmem_limit_bytes=32 * 2**20),
        name="exchange",
    )(velocity, edge_weights(columns))

    lines = cells * planes
    tiles = columns // TILE
    plane = pl.BlockSpec((cells, 1, planes, columns), lambda c: (0, c, 0, 0))
    deriv_x, deriv_y = pl.pallas_call(
        functools.partial(derive, ny),
        grid=(comps,),
        out_shape=[jax.ShapeDtypeStruct(velocity.shape, f32)] * 2,
        in_specs=[
            pl.BlockSpec(memory_space=pltpu.SMEM),
            plane,
            pl.BlockSpec((2, 1, planes, columns), lambda c: (0, c, 0, 0)),
            pl.BlockSpec((2, 2, 1, planes, columns), lambda c: (0, 0, c, 0, 0)),
            pl.BlockSpec((ny, cells, 1, planes, TILE), lambda c: (0, 0, c, 0, 0)),
            pl.BlockSpec((1, columns), lambda c: (0, 0)),
            pl.BlockSpec((3 * TILE, 3 * TILE), lambda c: (0, 0)),
        ],
        out_specs=[plane, plane],
        scratch_shapes=[
            pltpu.VMEM((min(8, tiles) * lines, 3 * TILE), jnp.bfloat16),
            pltpu.VMEM((tiles * lines, 3 * TILE), f32),
        ],
        compiler_params=pltpu.CompilerParams(vmem_limit_bytes=40 * 2**20),
        name="derive",
    )(metric_x, velocity, ein, halo, ygot, metric_y[None, :], y_tables())
    return deriv_x, deriv_y


def solution(mesh):
    placed = (P("gx", None, None, "gy"), P("gx"), P("gy"))
    return jax.shard_map(
        functools.partial(body, mesh.shape["gx"], mesh.shape["gy"]),
        mesh=mesh,
        in_specs=placed,
        out_specs=(P("gx", None, None, "gy"), P("gx", None, None, "gy")),
        check_vma=False,
    )
```

```python
import functools
import math

import jax
import jax.numpy as jnp
import numpy as np
from jax import lax
from jax.experimental import pallas as pl
from jax.experimental.pallas import tpu as pltpu
from jax.sharding import PartitionSpec as P

ALPHA = 0.49
COEF = {1: 949.0 / 1200.0, 2: 167.0 / 1500.0, 3: -47.0 / 6000.0}
RATIO = (1.0 - math.sqrt(1.0 - 4.0 * ALPHA * ALPHA)) / (2.0 * ALPHA)
RHO = -RATIO
LEADING = 1.0 / (1.0 - 2.0 * ALPHA * RATIO)
MESH = pl.DeviceIdType.MESH
TILE = 128
PARTS = 2


def power(count):
    return float(RHO**count)


def response(offset):
    green = lambda n: LEADING * RHO ** abs(n)
    return sum(w * (green(offset - k) - green(offset + k)) for k, w in COEF.items())


WAVE = response(3) / RHO**2
BAND1 = response(1) - WAVE
BAND2 = response(2) - WAVE * RHO


def y_tables():
    own, up, down = (np.zeros((TILE, TILE)) for _ in range(3))
    for j in range(TILE):
        for l in range(TILE):
            own[j, l] = response(j - l)
            up[j, l] = response(j - TILE - l)
            down[j, l] = response(j + TILE - l)
    table = np.concatenate((own, up, down), 1)
    high = table.astype(jnp.bfloat16)
    low = (table - high.astype(np.float64)).astype(jnp.bfloat16)
    return np.concatenate((high, high, low), 0)


def signed_power(count):
    size = jnp.exp(count.astype(jnp.float32) * math.log(RATIO))
    return jnp.where(count % 2 == 0, size, -size)


def exchange(nx, ny, v, ein, ygot, vbuf, esend, erecv, ssend, first, last, ysend,
             load_sem, edge_sem, own_sem, e_s, e_r, s_s, s_r, y_s, y_r):
    cells, comps, planes, columns = v.shape
    width = columns // nx
    x, y = lax.axis_index("gx"), lax.axis_index("gy")

    def target(q):
        return lax.rem(x + 1 + q, nx)

    def load(q):
        at = pl.multiple_of(target(q) * width, TILE)
        return pltpu.make_async_copy(v.at[:, :, :, pl.ds(at, width)], vbuf.at[q % 2], load_sem.at[q % 2])

    load(0).start()
    edges = [
        pltpu.make_async_copy(v.at[:, :, :, pl.ds(0, TILE)], first, edge_sem.at[0]),
        pltpu.make_async_copy(v.at[:, :, :, pl.ds(columns - TILE, TILE)], last, edge_sem.at[1]),
    ]
    for copy in edges:
        copy.start()
    barrier = pltpu.get_barrier_semaphore()
    for q in range(nx - 1):
        pl.semaphore_signal(barrier, inc=1, device_id=(target(q), y), device_id_type=MESH)
    for q in range(ny - 1):
        pl.semaphore_signal(barrier, inc=1, device_id=(x, lax.rem(y + 1 + q, ny)), device_id_type=MESH)
    pl.semaphore_wait(barrier, nx + ny - 2)

    sends = []
    to_low = jnp.zeros((cells, comps, planes, TILE), jnp.float32)
    to_high = jnp.zeros((cells, comps, planes, TILE), jnp.float32)
    ysum = [to_low, to_high]
    for q in range(nx):
        load(q).wait()
        if q + 1 < nx:
            load(q + 1).start()
        block = vbuf.at[q % 2]
        goes = esend.at[q] if q < nx - 1 else erecv.at[q]
        low, high = block[cells - 1], block[0]
        for i in range(1, cells):
            low = block[cells - 1 - i] + RHO * low
            high = block[i] + RHO * high
        goes[0] = low
        goes[1] = high
        if q < nx - 1:
            copy = pltpu.make_async_remote_copy(
                esend.at[q], erecv.at[q], e_s.at[q], e_r.at[q],
                device_id=(target(q), y), device_id_type=MESH)
            copy.start()
            sends.append(copy)
        start = target(q) * width
        for t in range(width // TILE):
            at = start + t * TILE
            part = block[:, :, :, t * TILE : (t + 1) * TILE]
            cell = at + lax.broadcasted_iota(jnp.int32, (1, 1, 1, TILE), 3)
            for side, away in enumerate((cell, columns - 1 - cell)):
                ysum[side] = ysum[side] + part * signed_power(away)

    for copy in edges:
        copy.wait()
    lane = lax.broadcasted_iota(jnp.int32, (cells, comps, planes, TILE), 3)
    sums = [jnp.sum(part, axis=3, keepdims=True) for part in ysum]
    message = jnp.where(lane < 2, first[...], jnp.where(lane >= TILE - 2, last[...], 0.0))
    message = jnp.where(lane == 2, sums[0], jnp.where(lane == 3, sums[1], message))
    ysend[...] = message
    for q in range(ny - 1):
        copy = pltpu.make_async_remote_copy(
            ysend, ygot.at[q], y_s.at[q], y_r.at[q],
            device_id=(x, lax.rem(y + 1 + q, ny)), device_id_type=MESH)
        copy.start()
        sends.append(copy)
    own_y = pltpu.make_async_copy(ysend, ygot.at[ny - 1], own_sem.at[0])
    own_y.start()

    for copy in sends[: nx - 1]:
        copy.wait_recv()
    closing = 1.0 / (1.0 - power(cells * nx))
    spot = pl.multiple_of(x * width, TILE)
    for q in range(nx):
        from_low, from_high = 0.0, 0.0
        for s in range(nx):
            ahead = (q + s + 1) % nx + 1
            behind = (-(q + s + 2) - 1) % nx + 1
            from_low = from_low + closing * power(cells * (ahead - 1)) * erecv[s, 1]
            from_high = from_high + closing * power(cells * (behind - 1)) * erecv[s, 0]
        ssend[q, 0] = from_low
        ssend[q, 1] = from_high
        place = ein.at[:, :, :, pl.ds(spot, width)]
        if q < nx - 1:
            copy = pltpu.make_async_remote_copy(
                ssend.at[q], place, s_s.at[q], s_r.at[q],
                device_id=(target(q), y), device_id_type=MESH)
            copy.start()
            sends.append(copy)
        else:
            own_x = pltpu.make_async_copy(ssend.at[q], place, own_sem.at[1])
            own_x.start()
    own_y.wait()
    own_x.wait()
    for copy in sends[: nx - 1]:
        copy.wait_send()
    for copy in sends[nx - 1 : nx + ny - 2]:
        copy.wait()
    for q, copy in enumerate(sends[nx + ny - 2 :]):
        copy.wait_send()
        at = pl.multiple_of(lax.rem(x + nx - 1 - q, nx) * width, TILE)
        pltpu.make_async_remote_copy(
            ssend.at[q], ein.at[:, :, :, pl.ds(at, width)], s_s.at[q], s_r.at[q],
            device_id=(target(q), y), device_id_type=MESH).wait_recv()


def derive_x(mx, v, ein, low, high, *rest):
    dx = rest[-1]
    cells, _, planes, columns = v.shape
    wide = 2 * TILE

    @pl.loop(0, columns // wide)
    def _(g):
        at = pl.ds(pl.multiple_of(g * wide, wide), wide)
        row = lambda i: (
            v[i, 0, :, at] if 0 <= i < cells
            else low[2 + i, 0, :, at] if i < 0
            else high[i - cells, 0, :, at])
        above = [None] * cells
        above[cells - 1] = ein[1, 0, :, at]
        for i in range(cells - 1, 0, -1):
            above[i - 1] = row(i) + RHO * above[i]
        below = ein[0, 0, :, at]
        for i in range(cells):
            line = WAVE * (above[i] - below) + BAND1 * (row(i + 1) - row(i - 1))
            line = line + BAND2 * (row(i + 2) - row(i - 2))
            dx[i, 0, :, at] = mx[i] * line
            below = row(i) + RHO * below

def derive_y(ny, v, ygot, my, table, dy, lhs, prod):
    cells, _, planes, columns = v.shape
    lines = cells * planes
    tiles = columns // TILE

    def flat(part):
        return part.reshape(lines, TILE)

    group = min(8, tiles)

    @pl.loop(0, tiles // group)
    def _(g):
        for t in range(group):
            at = pl.multiple_of((g * group + t) * TILE, TILE)
            part = flat(v[:, 0, :, pl.ds(at, TILE)])
            high = part.astype(jnp.bfloat16)
            low = (part - high.astype(jnp.float32)).astype(jnp.bfloat16)
            lhs[t * lines : (t + 1) * lines, 0:TILE] = high
            lhs[t * lines : (t + 1) * lines, TILE : 2 * TILE] = low
            lhs[t * lines : (t + 1) * lines, 2 * TILE :] = high
        rows = group * lines
        prod[pl.ds(pl.multiple_of(g * rows, rows), rows), :] = jnp.dot(
            lhs[...], table[...], preferred_element_type=jnp.float32)

    lane = lax.broadcasted_iota(jnp.int32, (1, TILE), 1)
    away = lane.astype(jnp.float32)
    sign = jnp.where(lane % 2 == 0, 1.0, -1.0).astype(jnp.float32)
    rise = WAVE * sign * jnp.exp(away * math.log(RATIO))
    fall = WAVE * -sign * jnp.exp((TILE - 1 - away) * math.log(RATIO))
    fall = -fall if TILE % 2 else fall
    step = power(columns)
    closing = 1.0 / (1.0 - power(columns * ny))
    low_in, high_in = 0.0, 0.0
    for s in range(ny):
        got = flat(ygot[s, :, 0])
        ahead = s + 1
        behind = ny - 1 - s if s < ny - 1 else ny
        low_in = low_in + closing * step ** (ahead - 1) * got[:, 3:4]
        high_in = high_in + closing * step ** (behind - 1) * got[:, 2:3]
    before = flat(ygot[0, :, 0])[:, TILE - 2 :]
    after = flat(ygot[ny - 2, :, 0])[:, 0:2]
    jump = power(TILE)

    def at_lane(n, value):
        return jnp.where(lane == n, value, 0.0)

    highs = [None] * tiles
    far = high_in
    for k in range(tiles - 1, -1, -1):
        highs[k] = far
        if k:
            seen = prod[k * lines : (k + 1) * lines, 3 * TILE - 3 : 3 * TILE - 2]
            far = seen * (1.0 / (WAVE * RHO**2)) + jump * far
    far = low_in
    for k in range(tiles):
        rows = slice(k * lines, (k + 1) * lines)
        line = prod[rows, 0:TILE]
        if k:
            line = line + prod[(k - 1) * lines : k * lines, TILE : 2 * TILE]
            line = line - (jump * past) * rise
        else:
            line = line - far * rise
            line = line - at_lane(0, BAND1 * before[:, 1:2] + BAND2 * before[:, 0:1])
            line = line - at_lane(1, BAND2 * before[:, 1:2])
        if k < tiles - 1:
            line = line + prod[(k + 1) * lines : (k + 2) * lines, 2 * TILE :]
            line = line + (jump * highs[k + 1]) * fall
        else:
            line = line + highs[k] * fall
            line = line + at_lane(TILE - 1, BAND1 * after[:, 0:1] + BAND2 * after[:, 1:2])
            line = line + at_lane(TILE - 2, BAND2 * after[:, 0:1])
        at = slice(k * TILE, (k + 1) * TILE)
        dy[:, 0, :, at] = (line * my[:, at]).reshape(cells, planes, TILE)
        past = far
        seen = prod[rows, TILE + 2 : TILE + 3]
        far = seen * (-1.0 / (WAVE * RHO**2)) + jump * past


def body(nx, ny, velocity, metric_x, metric_y):
    cells, comps, planes, columns = velocity.shape
    width = columns // nx
    part = columns // PARTS
    f32 = jnp.float32
    dma = pltpu.SemaphoreType.DMA
    hbm = pl.BlockSpec(memory_space=pl.ANY)
    up = [(i, (i + 1) % nx) for i in range(nx)]
    down = [(i, (i - 1) % nx) for i in range(nx)]
    rims = []
    for p in range(PARTS):
        here = velocity[:, :, :, p * part : (p + 1) * part]
        rims.append((lax.ppermute(here[cells - 2 :], "gx", up), lax.ppermute(here[:2], "gx", down)))
    ein, ygot = pl.pallas_call(
        functools.partial(exchange, nx, ny),
        out_shape=[
            jax.ShapeDtypeStruct((2, comps, planes, columns), f32),
            jax.ShapeDtypeStruct((ny, cells, comps, planes, TILE), f32),
        ],
        in_specs=[hbm],
        out_specs=[hbm, hbm],
        scratch_shapes=[
            pltpu.VMEM((2, cells, comps, planes, width), f32),
            pltpu.VMEM((nx, 2, comps, planes, width), f32),
            pltpu.VMEM((nx, 2, comps, planes, width), f32),
            pltpu.VMEM((nx, 2, comps, planes, width), f32),
            pltpu.VMEM((cells, comps, planes, TILE), f32),
            pltpu.VMEM((cells, comps, planes, TILE), f32),
            pltpu.VMEM((cells, comps, planes, TILE), f32),
            dma((2,)), dma((2,)), dma((2,)),
            dma((nx,)), dma((nx,)), dma((nx,)), dma((nx,)), dma((ny,)), dma((ny,)),
        ],
        compiler_params=pltpu.CompilerParams(
            collective_id=0, has_side_effects=True, vmem_limit_bytes=32 * 2**20),
        cost_estimate=pl.CostEstimate(
            flops=8 * velocity.size, bytes_accessed=4 * velocity.size, transcendentals=0),
        name="exchange",
    )(velocity)

    lines = cells * planes
    tiles = columns // TILE
    both = pl.CostEstimate(
        flops=20 * velocity.size, bytes_accessed=8 * velocity.size, transcendentals=0)
    plane = pl.BlockSpec((cells, 1, planes, columns), lambda c: (0, c, 0, 0))
    deriv_y = pl.pallas_call(
        functools.partial(derive_y, ny),
        grid=(comps,),
        out_shape=jax.ShapeDtypeStruct(velocity.shape, f32),
        in_specs=[
            plane,
            pl.BlockSpec((ny, cells, 1, planes, TILE), lambda c: (0, 0, c, 0, 0)),
            pl.BlockSpec((1, columns), lambda c: (0, 0)),
            pl.BlockSpec((3 * TILE, 3 * TILE), lambda c: (0, 0)),
        ],
        out_specs=plane,
        scratch_shapes=[
            pltpu.VMEM((min(8, tiles) * lines, 3 * TILE), jnp.bfloat16),
            pltpu.VMEM((tiles * lines, 3 * TILE), f32),
        ],
        compiler_params=pltpu.CompilerParams(vmem_limit_bytes=32 * 2**20),
        cost_estimate=both,
        name="derive_y",
    )(velocity, ygot, metric_y[None, :], y_tables())

    deriv_x = None
    for p in range(PARTS):
        spread = lambda c, p=p: (0, c, 0, p)
        whole = lambda c: (0, c, 0, 0)
        operands = [metric_x, velocity, ein, *rims[p]]
        specs = [
            pl.BlockSpec(memory_space=pltpu.SMEM),
            pl.BlockSpec((cells, 1, planes, part), spread),
            pl.BlockSpec((2, 1, planes, part), spread),
            pl.BlockSpec((2, 1, planes, part), whole),
            pl.BlockSpec((2, 1, planes, part), whole),
        ]
        if p:
            operands.append(deriv_x)
            specs.append(hbm)
        deriv_x = pl.pallas_call(
            derive_x,
            grid=(comps,),
            out_shape=jax.ShapeDtypeStruct(velocity.shape, f32),
            in_specs=specs,
            out_specs=pl.BlockSpec((cells, 1, planes, part), spread),
            input_output_aliases={5: 0} if p else {},
            compiler_params=pltpu.CompilerParams(vmem_limit_bytes=24 * 2**20),
            cost_estimate=pl.CostEstimate(
                flops=both.flops // PARTS, bytes_accessed=both.bytes_accessed // PARTS, transcendentals=0),
            name=f"derive_x{p}",
        )(*operands)
    return deriv_x, deriv_y


def solution(mesh):
    placed = (P("gx", None, None, "gy"), P("gx"), P("gy"))
    return jax.shard_map(
        functools.partial(body, mesh.shape["gx"], mesh.shape["gy"]),
        mesh=mesh,
        in_specs=placed,
        out_specs=(P("gx", None, None, "gy"), P("gx", None, None, "gy")),
        check_vma=False,
    )
```

```python
import functools
import math

import jax
import jax.numpy as jnp
import numpy as np
from jax import lax
from jax.experimental import pallas as pl
from jax.experimental.pallas import tpu as pltpu
from jax.sharding import PartitionSpec as P

ALPHA = 0.49
COEF = {1: 949.0 / 1200.0, 2: 167.0 / 1500.0, 3: -47.0 / 6000.0}
RATIO = (1.0 - math.sqrt(1.0 - 4.0 * ALPHA * ALPHA)) / (2.0 * ALPHA)
RHO = -RATIO
LEADING = 1.0 / (1.0 - 2.0 * ALPHA * RATIO)
MESH = pl.DeviceIdType.MESH
TILE = 128
PARTS = 4
FIRST = (4, 8)


def power(count):
    return float(RHO**count)


def response(offset):
    green = lambda n: LEADING * RHO ** abs(n)
    return sum(w * (green(offset - k) - green(offset + k)) for k, w in COEF.items())


WAVE = response(3) / RHO**2
BAND1 = response(1) - WAVE
BAND2 = response(2) - WAVE * RHO


def y_tables():
    own, up, down = (np.zeros((TILE, TILE)) for _ in range(3))
    for j in range(TILE):
        for l in range(TILE):
            own[j, l] = response(j - l)
            up[j, l] = response(j - TILE - l)
            down[j, l] = response(j + TILE - l)
    table = np.concatenate((own, up, down), 1)
    high = table.astype(jnp.bfloat16)
    low = (table - high.astype(np.float64)).astype(jnp.bfloat16)
    return np.concatenate((high, high, low), 0)


def signed_power(count):
    size = jnp.exp(count.astype(jnp.float32) * math.log(RATIO))
    return jnp.where(count % 2 == 0, size, -size)


def exchange(nx, ny, v, ein, halo, ygot, vbuf, esend, erecv, ssend, first, last, ysend,
             load_sem, edge_sem, own_sem, halo_send, halo_recv, e_s, e_r, s_s, s_r, y_s, y_r):
    cells, comps, planes, columns = v.shape
    width = columns // nx
    x, y = lax.axis_index("gx"), lax.axis_index("gy")

    def target(q):
        return lax.rem(x + 1 + q, nx)

    def load(q):
        at = pl.multiple_of(target(q) * width, TILE)
        return pltpu.make_async_copy(v.at[:, :, :, pl.ds(at, width)], vbuf.at[q % 2], load_sem.at[q % 2])

    load(0).start()
    edges = [
        pltpu.make_async_copy(v.at[:, :, :, pl.ds(0, TILE)], first, edge_sem.at[0]),
        pltpu.make_async_copy(v.at[:, :, :, pl.ds(columns - TILE, TILE)], last, edge_sem.at[1]),
    ]
    for copy in edges:
        copy.start()
    barrier = pltpu.get_barrier_semaphore()
    for q in range(nx - 1):
        pl.semaphore_signal(barrier, inc=1, device_id=(target(q), y), device_id_type=MESH)
    for q in range(ny - 1):
        pl.semaphore_signal(barrier, inc=1, device_id=(x, lax.rem(y + 1 + q, ny)), device_id_type=MESH)
    pl.semaphore_wait(barrier, nx + ny - 2)

    right, left = lax.rem(x + 1, nx), lax.rem(x + nx - 1, nx)
    piece = columns // PARTS
    rims = []
    for p in range(PARTS):
        at = slice(p * piece, (p + 1) * piece)
        rims += [
            pltpu.make_async_remote_copy(
                v.at[cells - 2 :, :, :, at], halo.at[0, :, :, :, at], halo_send.at[2 * p], halo_recv.at[2 * p],
                device_id=(right, y), device_id_type=MESH),
            pltpu.make_async_remote_copy(
                v.at[:2, :, :, at], halo.at[1, :, :, :, at], halo_send.at[2 * p + 1], halo_recv.at[2 * p + 1],
                device_id=(left, y), device_id_type=MESH),
        ]
    cuts = [0, *FIRST, 2 * PARTS]
    begin = lambda n: [copy.start() for copy in rims[cuts[n] : cuts[n + 1]]]

    begin(0)
    sends = []
    to_low = jnp.zeros((cells, comps, planes, TILE), jnp.float32)
    to_high = jnp.zeros((cells, comps, planes, TILE), jnp.float32)
    ysum = [to_low, to_high]
    for q in range(nx):
        load(q).wait()
        if q + 1 < nx:
            load(q + 1).start()
        block = vbuf.at[q % 2]
        goes = esend.at[q] if q < nx - 1 else erecv.at[q]
        low, high = block[cells - 1], block[0]
        for i in range(1, cells):
            low = block[cells - 1 - i] + RHO * low
            high = block[i] + RHO * high
        goes[0] = low
        goes[1] = high
        if q < nx - 1:
            copy = pltpu.make_async_remote_copy(
                esend.at[q], erecv.at[q], e_s.at[q], e_r.at[q],
                device_id=(target(q), y), device_id_type=MESH)
            copy.start()
            sends.append(copy)
        start = target(q) * width
        for t in range(width // TILE):
            at = start + t * TILE
            part = block[:, :, :, t * TILE : (t + 1) * TILE]
            cell = at + lax.broadcasted_iota(jnp.int32, (1, 1, 1, TILE), 3)
            for side, away in enumerate((cell, columns - 1 - cell)):
                ysum[side] = ysum[side] + part * signed_power(away)

    begin(1)
    for copy in edges:
        copy.wait()
    lane = lax.broadcasted_iota(jnp.int32, (cells, comps, planes, TILE), 3)
    sums = [jnp.sum(part, axis=3, keepdims=True) for part in ysum]
    message = jnp.where(lane < 2, first[...], jnp.where(lane >= TILE - 2, last[...], 0.0))
    message = jnp.where(lane == 2, sums[0], jnp.where(lane == 3, sums[1], message))
    ysend[...] = message
    for q in range(ny - 1):
        copy = pltpu.make_async_remote_copy(
            ysend, ygot.at[q], y_s.at[q], y_r.at[q],
            device_id=(x, lax.rem(y + 1 + q, ny)), device_id_type=MESH)
        copy.start()
        sends.append(copy)
    own_y = pltpu.make_async_copy(ysend, ygot.at[ny - 1], own_sem.at[0])
    own_y.start()

    for copy in sends[: nx - 1]:
        copy.wait_recv()
    closing = 1.0 / (1.0 - power(cells * nx))
    spot = pl.multiple_of(x * width, TILE)
    for q in range(nx):
        from_low, from_high = 0.0, 0.0
        for s in range(nx):
            ahead = (q + s + 1) % nx + 1
            behind = (-(q + s + 2) - 1) % nx + 1
            from_low = from_low + closing * power(cells * (ahead - 1)) * erecv[s, 1]
            from_high = from_high + closing * power(cells * (behind - 1)) * erecv[s, 0]
        ssend[q, 0] = from_low
        ssend[q, 1] = from_high
        place = ein.at[:, :, :, pl.ds(spot, width)]
        if q < nx - 1:
            copy = pltpu.make_async_remote_copy(
                ssend.at[q], place, s_s.at[q], s_r.at[q],
                device_id=(target(q), y), device_id_type=MESH)
            copy.start()
            sends.append(copy)
        else:
            own_x = pltpu.make_async_copy(ssend.at[q], place, own_sem.at[1])
            own_x.start()
    begin(2)
    own_y.wait()
    own_x.wait()
    for copy in rims:
        copy.wait()
    for copy in sends[: nx - 1]:
        copy.wait_send()
    for copy in sends[nx - 1 : nx + ny - 2]:
        copy.wait()
    for q, copy in enumerate(sends[nx + ny - 2 :]):
        copy.wait_send()
        at = pl.multiple_of(lax.rem(x + nx - 1 - q, nx) * width, TILE)
        pltpu.make_async_remote_copy(
            ssend.at[q], ein.at[:, :, :, pl.ds(at, width)], s_s.at[q], s_r.at[q],
            device_id=(target(q), y), device_id_type=MESH).wait_recv()


def derive(ny, mx, v, ein, halo, ygot, my, table, dx, dy, lhs, prod):
    cells, _, planes, columns = v.shape
    lines = cells * planes
    tiles = columns // TILE

    def flat(part):
        return part.reshape(lines, TILE)

    group = min(8, tiles)

    @pl.loop(0, tiles // group)
    def _(g):
        for t in range(group):
            at = pl.multiple_of((g * group + t) * TILE, TILE)
            part = flat(v[:, 0, :, pl.ds(at, TILE)])
            high = part.astype(jnp.bfloat16)
            low = (part - high.astype(jnp.float32)).astype(jnp.bfloat16)
            lhs[t * lines : (t + 1) * lines, 0:TILE] = high
            lhs[t * lines : (t + 1) * lines, TILE : 2 * TILE] = low
            lhs[t * lines : (t + 1) * lines, 2 * TILE :] = high
        rows = group * lines
        prod[pl.ds(pl.multiple_of(g * rows, rows), rows), :] = jnp.dot(
            lhs[...], table[...], preferred_element_type=jnp.float32)

    wide = 2 * TILE

    @pl.loop(0, columns // wide)
    def _(g):
        at = pl.ds(pl.multiple_of(g * wide, wide), wide)
        row = lambda i: (
            v[i, 0, :, at] if 0 <= i < cells
            else halo[0, 2 + i, 0, :, at] if i < 0
            else halo[1, i - cells, 0, :, at])
        above = [None] * cells
        above[cells - 1] = ein[1, 0, :, at]
        for i in range(cells - 1, 0, -1):
            above[i - 1] = row(i) + RHO * above[i]
        below = ein[0, 0, :, at]
        for i in range(cells):
            line = WAVE * (above[i] - below) + BAND1 * (row(i + 1) - row(i - 1))
            line = line + BAND2 * (row(i + 2) - row(i - 2))
            dx[i, 0, :, at] = mx[i] * line
            below = row(i) + RHO * below

    lane = lax.broadcasted_iota(jnp.int32, (1, TILE), 1)
    away = lane.astype(jnp.float32)
    sign = jnp.where(lane % 2 == 0, 1.0, -1.0).astype(jnp.float32)
    rise = WAVE * sign * jnp.exp(away * math.log(RATIO))
    fall = WAVE * -sign * jnp.exp((TILE - 1 - away) * math.log(RATIO))
    fall = -fall if TILE % 2 else fall
    step = power(columns)
    closing = 1.0 / (1.0 - power(columns * ny))
    low_in, high_in = 0.0, 0.0
    for s in range(ny):
        got = flat(ygot[s, :, 0])
        ahead = s + 1
        behind = ny - 1 - s if s < ny - 1 else ny
        low_in = low_in + closing * step ** (ahead - 1) * got[:, 3:4]
        high_in = high_in + closing * step ** (behind - 1) * got[:, 2:3]
    before = flat(ygot[0, :, 0])[:, TILE - 2 :]
    after = flat(ygot[ny - 2, :, 0])[:, 0:2]
    jump = power(TILE)

    def at_lane(n, value):
        return jnp.where(lane == n, value, 0.0)

    highs = [None] * tiles
    far = high_in
    for k in range(tiles - 1, -1, -1):
        highs[k] = far
        if k:
            seen = prod[k * lines : (k + 1) * lines, 3 * TILE - 3 : 3 * TILE - 2]
            far = seen * (1.0 / (WAVE * RHO**2)) + jump * far
    far = low_in
    for k in range(tiles):
        rows = slice(k * lines, (k + 1) * lines)
        line = prod[rows, 0:TILE]
        if k:
            line = line + prod[(k - 1) * lines : k * lines, TILE : 2 * TILE]
            line = line - (jump * past) * rise
        else:
            line = line - far * rise
            line = line - at_lane(0, BAND1 * before[:, 1:2] + BAND2 * before[:, 0:1])
            line = line - at_lane(1, BAND2 * before[:, 1:2])
        if k < tiles - 1:
            line = line + prod[(k + 1) * lines : (k + 2) * lines, 2 * TILE :]
            line = line + (jump * highs[k + 1]) * fall
        else:
            line = line + highs[k] * fall
            line = line + at_lane(TILE - 1, BAND1 * after[:, 0:1] + BAND2 * after[:, 1:2])
            line = line + at_lane(TILE - 2, BAND2 * after[:, 0:1])
        at = slice(k * TILE, (k + 1) * TILE)
        dy[:, 0, :, at] = (line * my[:, at]).reshape(cells, planes, TILE)
        past = far
        seen = prod[rows, TILE + 2 : TILE + 3]
        far = seen * (-1.0 / (WAVE * RHO**2)) + jump * past


def body(nx, ny, velocity, metric_x, metric_y):
    cells, comps, planes, columns = velocity.shape
    width = columns // nx
    f32 = jnp.float32
    dma = pltpu.SemaphoreType.DMA
    hbm = pl.BlockSpec(memory_space=pl.ANY)
    ein, halo, ygot = pl.pallas_call(
        functools.partial(exchange, nx, ny),
        out_shape=[
            jax.ShapeDtypeStruct((2, comps, planes, columns), f32),
            jax.ShapeDtypeStruct((2, 2, comps, planes, columns), f32),
            jax.ShapeDtypeStruct((ny, cells, comps, planes, TILE), f32),
        ],
        in_specs=[hbm],
        out_specs=[hbm, hbm, hbm],
        scratch_shapes=[
            pltpu.VMEM((2, cells, comps, planes, width), f32),
            pltpu.VMEM((nx, 2, comps, planes, width), f32),
            pltpu.VMEM((nx, 2, comps, planes, width), f32),
            pltpu.VMEM((nx, 2, comps, planes, width), f32),
            pltpu.VMEM((cells, comps, planes, TILE), f32),
            pltpu.VMEM((cells, comps, planes, TILE), f32),
            pltpu.VMEM((cells, comps, planes, TILE), f32),
            dma((2,)), dma((2,)), dma((2,)), dma((2 * PARTS,)), dma((2 * PARTS,)),
            dma((nx,)), dma((nx,)), dma((nx,)), dma((nx,)), dma((ny,)), dma((ny,)),
        ],
        compiler_params=pltpu.CompilerParams(
            collective_id=0, has_side_effects=True, vmem_limit_bytes=32 * 2**20),
        name="exchange",
    )(velocity)

    lines = cells * planes
    tiles = columns // TILE
    plane = pl.BlockSpec((cells, 1, planes, columns), lambda c: (0, c, 0, 0))
    deriv_x, deriv_y = pl.pallas_call(
        functools.partial(derive, ny),
        grid=(comps,),
        out_shape=[jax.ShapeDtypeStruct(velocity.shape, f32)] * 2,
        in_specs=[
            pl.BlockSpec(memory_space=pltpu.SMEM),
            plane,
            pl.BlockSpec((2, 1, planes, columns), lambda c: (0, c, 0, 0)),
            pl.BlockSpec((2, 2, 1, planes, columns), lambda c: (0, 0, c, 0, 0)),
            pl.BlockSpec((ny, cells, 1, planes, TILE), lambda c: (0, 0, c, 0, 0)),
            pl.BlockSpec((1, columns), lambda c: (0, 0)),
            pl.BlockSpec((3 * TILE, 3 * TILE), lambda c: (0, 0)),
        ],
        out_specs=[plane, plane],
        scratch_shapes=[
            pltpu.VMEM((min(8, tiles) * lines, 3 * TILE), jnp.bfloat16),
            pltpu.VMEM((tiles * lines, 3 * TILE), f32),
        ],
        compiler_params=pltpu.CompilerParams(vmem_limit_bytes=40 * 2**20),
        name="derive",
    )(metric_x, velocity, ein, halo, ygot, metric_y[None, :], y_tables())
    return deriv_x, deriv_y


def solution(mesh):
    placed = (P("gx", None, None, "gy"), P("gx"), P("gy"))
    return jax.shard_map(
        functools.partial(body, mesh.shape["gx"], mesh.shape["gy"]),
        mesh=mesh,
        in_specs=placed,
        out_specs=(P("gx", None, None, "gy"), P("gx", None, None, "gy")),
        check_vma=False,
    )
```
